32 devices in a mesh: pts: 16 (over z, y, core), grp: 2 (over x).
Axes of the slice: x: 2, y: 2, z: 4, core: 2. Of those that a mesh axis runs over, the one named last changes fastest.
Arguments:
- occ_orbitals: bfloat16 [4096, 1024], P('pts'), may hold values from -0.1875 to 0.1875
- virt_orbitals: bfloat16 [4096, 1024], P('pts'), may hold values from -0.1875 to 0.1875
- columns: bfloat16 [4096, 512], P('pts'), may hold values from -6 to 6
- occ_energies: float32 [1024], replicated, may hold values from -3 to -0.1
- vir_energies: float32 [1024], replicated, may hold values from 0.1 to 3
- tau_index: int32 [8], replicated, may hold values from 0 to 15, as said below
- quad_weights: float32 [8], replicated, may hold values from 0.05 to 0.5
- frequencies: float32 [2], replicated, may hold values from 0.2 to 2
- distance_kept: int32 [16], replicated, may hold values 0 or 1
Outputs:
- response: float32 [2, 512, 4096], P(None, 'grp', 'pts')
The draws below stay inside these ranges and needn't reach their ends.
Inputs may be any that keep to these rules, and one draw needn't show every extreme that they name: `tau_index`: all entries differ; 0 and 15 are always among them.
All inputs are finite; a program needn't handle non-finite values.
Results may differ from the reference program's by a relative error of at most 0.0026.
Values may be sent and summed in bfloat16 or wider, within the bound.
A program may use at most 64 MiB of HBM per device.

```python
import math
import jax
import jax.numpy as jnp
from jax import lax

NOCC = 1024
NVIR = 1024
BP = 256
NCOL = 512
NTAU = 8
NGRID = 16
NFREQ = 2
NP = 4096
N_PTS = 16


def draw_tau_index(key, part):
    inner_key = jax.random.fold_in(key, 11)
    order_key = jax.random.fold_in(key, 23)
    middle = jax.random.permutation(inner_key, NGRID - 2)[:NTAU - 2].astype(jnp.int32) + 1
    chosen = jnp.concatenate([jnp.zeros((1,), jnp.int32), jnp.full((1,), NGRID - 1, jnp.int32), middle])
    return jax.random.permutation(order_key, chosen).astype(jnp.int32)


def with_ends(entries, stream_key, smallest, top_value):
    index_at = [jax.random.randint(jax.random.fold_in(stream_key, axis), (), 0, length) for axis, length in enumerate(entries.shape)]
    widest = entries.shape.index(max(entries.shape))
    beside = index_at[:widest] + [(index_at[widest] + 1) % entries.shape[widest]] + index_at[widest + 1:]
    return entries.at[tuple(index_at)].set(smallest).at[tuple(beside)].set(top_value)


def block_scale(stream_key, dims, cuts, least, high):
    loudness, own = 1.0, jax.random.fold_in(stream_key, 6)
    for position, parts in cuts:
        draws = jnp.exp(jax.random.uniform(jax.random.fold_in(own, position), (parts,), jnp.float32, least / len(cuts), high / len(cuts)))
        loudness = loudness * jnp.repeat(draws, dims[position] // parts).reshape([-1 if axis == position else 1 for axis in range(len(dims))])
    return loudness


def gaussian(rng, shape, deviation, bound, shards=(), kind=jnp.bfloat16):
    result = jax.random.normal(rng, shape, jnp.float32) * deviation
    if len(shards) > 0:
        result = block_scale(rng, shape, shards, -0.22, 0.18) * result
    return jnp.clip(result, min=-bound, max=bound).astype(kind)


def setup_inputs(seed: int = 0) -> dict:
    splits = jax.random.split(jax.random.key(seed), 10)
    occ_orbitals = gaussian(splits[0], (NP, NOCC), NOCC ** -0.5, 0.1875, ((0, 16),))
    virt_orbitals = gaussian(splits[1], (NP, NVIR), NVIR ** -0.5, 0.1875, ((0, 16),))
    columns = gaussian(splits[2], (NP, NCOL), 1.0, 6.0, ((0, 16),))
    occ_energies = jnp.clip(jax.random.uniform(splits[3], (NOCC,), jnp.float32, -3.0, -0.1), -3.0, -0.1)
    vir_energies = jnp.clip(jax.random.uniform(splits[4], (NVIR,), jnp.float32, 0.1, 3.0), 0.1, 3.0)
    tau_index = draw_tau_index(jax.random.fold_in(splits[9], 71), 0)
    quad_weights = jnp.clip(jnp.exp(jax.random.uniform(splits[6], (NTAU,), jnp.float32, math.log(0.05), math.log(0.5))), 0.05, 0.5)
    frequencies = jnp.clip(jnp.exp(jax.random.uniform(splits[7], (NFREQ,), jnp.float32, math.log(0.2), math.log(2.0))), 0.2, 2.0)
    distance_kept = with_ends((jax.random.randint(splits[8], (N_PTS,), 0, 4) < 3).astype(jnp.int32), jax.random.fold_in(splits[8], 1), 0, 1)
    return {"occ_orbitals": occ_orbitals, "virt_orbitals": virt_orbitals, "columns": columns, "occ_energies": occ_energies, "vir_energies": vir_energies, "tau_index": tau_index, "quad_weights": quad_weights, "frequencies": frequencies, "distance_kept": distance_kept}


def reference(occ_orbitals, virt_orbitals, columns, occ_energies, vir_energies, tau_index, quad_weights, frequencies, distance_kept):
    highest = lax.Precision.HIGHEST
    times = 0.05 * jnp.exp(tau_index.astype(jnp.float32) * jnp.float32(math.log(1.5)))
    cosine = -quad_weights[None, :] * jnp.cos(frequencies[:, None] * times[None, :])
    occ_full = occ_orbitals.astype(jnp.float32)
    vir_full = virt_orbitals.astype(jnp.float32)
    col_full = columns.astype(jnp.float32)
    occ_blocks = occ_full.reshape(N_PTS, BP, NOCC)
    vir_blocks = vir_full.reshape(N_PTS, BP, NVIR)
    col_block = jnp.arange(N_PTS * BP, dtype=jnp.int32) // BP
    occ_decay = jnp.exp(occ_energies[None, :] * times[:, None])
    vir_decay = jnp.exp(-vir_energies[None, :] * times[:, None])

    def one_block(carry, inputs):
        row_block, occ_rows, vir_rows = inputs
        occ_scaled = (occ_rows[None] * occ_decay[:, None, :]).astype(jnp.bfloat16).astype(jnp.float32)
        vir_scaled = (vir_rows[None] * vir_decay[:, None, :]).astype(jnp.bfloat16).astype(jnp.float32)
        green_occ = jnp.dot(occ_scaled.reshape(NTAU * BP, NOCC), occ_full.T, precision=highest, preferred_element_type=jnp.float32)
        green_vir = jnp.dot(vir_scaled.reshape(NTAU * BP, NVIR), vir_full.T, precision=highest, preferred_element_type=jnp.float32)
        product = (green_occ * green_vir).reshape(NTAU, BP, N_PTS * BP)
        chi = jnp.einsum("wk,krs->wrs", cosine, product, precision=highest)
        distance = (col_block - row_block) % N_PTS
        kept = distance_kept[distance].astype(jnp.float32)
        chi = chi * kept[None, None, :]
        answer = jnp.einsum("wrs,sc->wcr", chi, col_full, precision=highest)
        return carry, answer

    _, pieces = lax.scan(one_block, jnp.int32(0), (jnp.arange(N_PTS, dtype=jnp.int32), occ_blocks, vir_blocks))
    return jnp.transpose(pieces, (1, 2, 0, 3)).reshape(NFREQ, NCOL, N_PTS * BP)
```

```python
import functools
import math

import jax
import jax.numpy as jnp
from jax import lax
from jax.experimental import pallas as pl
from jax.experimental.pallas import tpu as pltpu
from jax.sharding import PartitionSpec as P

MESH = pl.DeviceIdType.MESH
NT = (((1,), (1,)), ((), ()))
F32, BF16 = jnp.float32, jnp.bfloat16
ROWS, CORES = 2, 2
DOWN, UP, ACROSS, BESIDE = range(4)
TIMES_AT_ONCE = 4


def kernel(
    cycle, groups,
    occ_ref, vir_ref, col_ref, occ_e_ref, vir_e_ref, tau_ref, weight_ref, freq_ref, kept_ref,
    out_ref,
    occ_s, vir_s, gathered, chi, total, turned, turned_sent, landed, cos_rows,
    send_sem, recv_sem, sum_send_sem, sum_recv_sem,
):
    me, grp = lax.axis_index("pts"), lax.axis_index("grp")
    layers = cycle // (ROWS * CORES)
    layer, row, core = me // (ROWS * CORES), (me // CORES) % ROWS, me % CORES
    points, n_occ = occ_ref.shape
    n_vir, n_col = vir_ref.shape[1], col_ref.shape[1]
    n_tau, n_freq = tau_ref.shape[0], freq_ref.shape[0]
    part = points // groups
    pair = CORES * part
    share = n_col // groups

    def index(a, b, c):
        return (a * ROWS + b) * CORES + c

    def move(slot, target, way):
        rows = pl.ds(pl.multiple_of(slot * part, part), part)
        return pltpu.make_async_remote_copy(
            src_ref=gathered.at[rows],
            dst_ref=gathered.at[rows],
            send_sem=send_sem.at[way, slot],
            recv_sem=recv_sem.at[slot],
            device_id={"pts": target},
            device_id_type=MESH,
        )

    below, above = index(layer - 1, row, core), index(layer + 1, row, core)
    across, beside = index(layer, 1 - row, core), index(layer, row, 1 - core)

    mine = pl.ds(pl.multiple_of(grp * part, part), part)
    own = pl.ds(pl.multiple_of(me * part, part), part)
    gathered[own, :n_occ] = occ_ref[mine]
    gathered[own, n_occ:n_occ + n_vir] = vir_ref[mine]
    gathered[own, n_occ + n_vir:] = col_ref[mine]

    barrier = pltpu.get_barrier_semaphore()

    def greet(**where):
        pl.semaphore_signal(barrier, inc=1, device_id=where, device_id_type=MESH)

    greet(pts=across)
    greet(pts=beside)
    for step in range(1, groups):
        greet(grp=lax.rem(grp + step, groups))

    @pl.when(layer > 0)
    def _():
        greet(pts=below)

    @pl.when(layer < layers - 1)
    def _():
        greet(pts=above)

    ends = (layer == 0).astype(jnp.int32) + (layer == layers - 1).astype(jnp.int32)
    pl.semaphore_wait(barrier, groups + 3 - ends)

    @pl.when(layer > 0)
    def _():
        move(me, below, DOWN).start()

    @pl.when(layer < layers - 1)
    def _():
        move(me, above, UP).start()

    move(me, across, ACROSS).start()
    move(me, beside, BESIDE).start()

    total[...] = jnp.zeros_like(total)

    def scale(k, _):
        index_row = jnp.full((1, n_occ), tau_ref[k].astype(F32), F32)
        time = 0.05 * jnp.exp(index_row * jnp.float32(math.log(1.5)))
        rows = pl.ds(pl.multiple_of(k * points, points), points)
        decay = jnp.exp(occ_e_ref[...].reshape(1, n_occ) * time)
        occ_s[rows] = (occ_ref[...].astype(F32) * decay).astype(BF16)
        index_row = jnp.full((1, n_vir), tau_ref[k].astype(F32), F32)
        time = 0.05 * jnp.exp(index_row * jnp.float32(math.log(1.5)))
        decay = jnp.exp(-vir_e_ref[...].reshape(1, n_vir) * time)
        vir_s[rows] = (vir_ref[...].astype(F32) * decay).astype(BF16)
        for w in range(n_freq):
            cos_rows[w, k] = -weight_ref[k] * jnp.cos(freq_ref[w] * time[:, :pair])
        return 0

    lax.fori_loop(0, n_tau, scale, 0)

    def compute(a, b):
        slot = index(a, b, 0)
        rows = pl.ds(pl.multiple_of(slot * part, pair), pair)
        block_tau = TIMES_AT_ONCE

        def some_times(i, _):
            at = pl.ds(pl.multiple_of(i * block_tau * points, block_tau * points), block_tau * points)
            green_occ = lax.dot_general(
                occ_s[at], gathered[rows, :n_occ], NT, preferred_element_type=F32
            )
            green_vir = lax.dot_general(
                vir_s[at], gathered[rows, n_occ:n_occ + n_vir], NT, preferred_element_type=F32
            )
            product = green_occ * green_vir
            for w in range(n_freq):
                added = 0.0
                for j in range(block_tau):
                    added += cos_rows[w, i * block_tau + j] * product[j * points:(j + 1) * points]

                @pl.when(i == 0)
                def _():
                    chi[w] = added

                @pl.when(i > 0)
                def _():
                    chi[w] += added
            return 0

        lax.fori_loop(0, n_tau // block_tau, some_times, 0)
        lane = lax.broadcasted_iota(jnp.int32, (1, pair), 1)
        kept = jnp.where(
            lane < part,
            kept_ref[lax.rem(slot - me + cycle, cycle)].astype(F32),
            kept_ref[lax.rem(slot + 1 - me + cycle, cycle)].astype(F32),
        )
        for w in range(n_freq):
            total[w] += jnp.dot(
                (chi[w] * kept).astype(BF16),
                gathered[rows, n_occ + n_vir:],
                preferred_element_type=F32,
            )

    def inside(a):
        return jnp.logical_and(a >= 0, a < layers)

    def same_row_arrives(t):
        for way in (-1, 1):
            @pl.when(inside(layer + way * t))
            def _():
                slot = index(layer + way * t, row, core)
                move(slot, me, DOWN).wait_recv()
                onward = layer - way

                @pl.when(inside(onward))
                def _():
                    move(slot, index(onward, row, core), DOWN if way > 0 else UP).start()

                move(slot, across, ACROSS).start()
                move(slot, beside, BESIDE).start()

    def other_row_arrives(t, ways):
        for way in ways:
            @pl.when(inside(layer + way * t))
            def _():
                slot = index(layer + way * t, 1 - row, core)
                move(slot, me, DOWN).wait_recv()
                move(slot, beside, BESIDE).start()

    def work(t, b, ways):
        for way in ways:
            @pl.when(inside(layer + way * t))
            def _():
                move(index(layer + way * t, b, 1 - core), me, DOWN).wait_recv()
                compute(layer + way * t, b)

    work(0, row, (1,))

    def round_(t, _):
        same_row_arrives(t)

        @pl.when(t == 1)
        def _():
            other_row_arrives(0, (1,))

        @pl.when(t > 1)
        def _():
            other_row_arrives(t - 1, (-1, 1))

        def one(n, _):
            other = n // 2
            gap = t - other
            place = layer + gap * (2 * (n % 2) - 1)
            fresh = jnp.logical_or(gap > 0, n % 2 == 1)

            @pl.when(jnp.logical_and(inside(place), fresh))
            def _():
                b = row + other * (1 - 2 * row)
                move(index(place, b, 1 - core), me, DOWN).wait_recv()
                compute(place, b)
            return 0

        lax.fori_loop(0, 4, one, 0)
        return 0

    lax.fori_loop(1, layers, round_, 0)
    other_row_arrives(layers - 1, (-1, 1))

    def last(n, _):
        place = layer + (layers - 1) * (2 * n - 1)

        @pl.when(inside(place))
        def _():
            move(index(place, 1 - row, 1 - core), me, DOWN).wait_recv()
            compute(place, 1 - row)
        return 0

    lax.fori_loop(0, 2, last, 0)

    for w in range(n_freq):
        flipped = total[w].T
        turned[w] = flipped
        turned_sent[w] = flipped.astype(BF16)
    sums = []
    for step in range(1, groups):
        to = lax.rem(grp + step, groups)
        sums.append(
            pltpu.make_async_remote_copy(
                src_ref=turned_sent.at[:, pl.ds(pl.multiple_of(to * share, share), share)],
                dst_ref=landed.at[step - 1],
                send_sem=sum_send_sem.at[step - 1],
                recv_sem=sum_recv_sem.at[step - 1],
                device_id={"grp": to},
                device_id_type=MESH,
            )
        )
        sums[-1].start()

    def left(slot, _):
        a, b, c = slot // (ROWS * CORES), (slot // CORES) % ROWS, slot % CORES
        mine_core = c == core
        same = jnp.logical_and(mine_core, b == row)

        @pl.when(jnp.logical_and(same, jnp.logical_and(a >= layer, layer > 0)))
        def _():
            move(slot, below, DOWN).wait_send()

        @pl.when(jnp.logical_and(same, jnp.logical_and(a <= layer, layer < layers - 1)))
        def _():
            move(slot, above, UP).wait_send()

        @pl.when(same)
        def _():
            move(slot, across, ACROSS).wait_send()

        @pl.when(mine_core)
        def _():
            move(slot, beside, BESIDE).wait_send()
        return 0

    lax.fori_loop(0, cycle, left, 0)
    for copy in sums:
        copy.wait()
    answer = turned[:, pl.ds(pl.multiple_of(grp * share, share), share)]
    for step in range(groups - 1):
        answer = answer + landed[step].astype(F32)
    out_ref[...] = answer


def per_device(occ, vir, col, occ_e, vir_e, tau, weights, frequencies, kept):
    cycle, groups = lax.axis_size("pts"), lax.axis_size("grp")
    points, n_occ = occ.shape
    n_vir, n_col = vir.shape[1], col.shape[1]
    n_tau, n_freq = tau.shape[0], frequencies.shape[0]
    part, share = points // groups, n_col // groups
    vmem = pl.BlockSpec(memory_space=pltpu.VMEM)
    smem = pl.BlockSpec(memory_space=pltpu.SMEM)
    return pl.pallas_call(
        functools.partial(kernel, cycle, groups),
        out_shape=jax.ShapeDtypeStruct((n_freq, share, points), F32),
        in_specs=[vmem] * 5 + [smem] * 4,
        out_specs=vmem,
        scratch_shapes=[
            pltpu.VMEM((n_tau * points, n_occ), BF16),
            pltpu.VMEM((n_tau * points, n_vir), BF16),
            pltpu.VMEM((cycle * part, n_occ + n_vir + n_col), BF16),
            pltpu.VMEM((n_freq, points, CORES * part), F32),
            pltpu.VMEM((n_freq, points, n_col), F32),
            pltpu.VMEM((n_freq, n_col, points), F32),
            pltpu.VMEM((n_freq, n_col, points), BF16),
            pltpu.VMEM((groups - 1, n_freq, share, points), BF16),
            pltpu.VMEM((n_freq, n_tau, 1, CORES * part), F32),
            pltpu.SemaphoreType.DMA((4, cycle)),
            pltpu.SemaphoreType.DMA((cycle,)),
            pltpu.SemaphoreType.DMA((groups - 1,)),
            pltpu.SemaphoreType.DMA((groups - 1,)),
        ],
        compiler_params=pltpu.CompilerParams(
            collective_id=0, has_side_effects=True, vmem_limit_bytes=56 * 1024 * 1024
        ),
    )(occ, vir, col, occ_e, vir_e, tau, weights, frequencies, kept)


def solution(mesh):
    placed = (P("pts", None), P("pts", None), P("pts", None), P(), P(), P(), P(), P(), P())
    return jax.shard_map(
        per_device, mesh=mesh, in_specs=placed, out_specs=P(None, "grp", "pts"), check_vma=False
    )
```

```python
import functools
import math

import jax
import jax.numpy as jnp
from jax import lax
from jax.experimental import pallas as pl
from jax.experimental.pallas import tpu as pltpu
from jax.sharding import PartitionSpec as P

MESH = pl.DeviceIdType.MESH
NT = (((1,), (1,)), ((), ()))
F32, BF16 = jnp.float32, jnp.bfloat16
ROWS, CORES = 2, 2
DOWN, UP, ACROSS, BESIDE = range(4)
PIECES = 2


def kernel(
    cycle, groups,
    occ_ref, vir_ref, col_ref, occ_e_ref, vir_e_ref, tau_ref, weight_ref, freq_ref, kept_ref,
    out_ref,
    occ_s, vir_s, gathered, green_occ, total, turned, turned_sent, landed, cos_rows,
    send_sem, recv_sem, sum_send_sem, sum_recv_sem,
):
    me, grp = lax.axis_index("pts"), lax.axis_index("grp")
    layers = cycle // (ROWS * CORES)
    layer, row, core = me // (ROWS * CORES), (me // CORES) % ROWS, me % CORES
    points, n_occ = occ_ref.shape
    n_vir, n_col = vir_ref.shape[1], col_ref.shape[1]
    n_tau, n_freq = tau_ref.shape[0], freq_ref.shape[0]
    part = points // groups
    pair = CORES * part
    share = n_col // groups

    def index(a, b, c):
        return (a * ROWS + b) * CORES + c

    piece = part // PIECES

    def move(slot, h, target, way):
        rows = pl.ds(pl.multiple_of(slot * part + h * piece, piece), piece)
        return pltpu.make_async_remote_copy(
            src_ref=gathered.at[rows],
            dst_ref=gathered.at[rows],
            send_sem=send_sem.at[way, slot, h],
            recv_sem=recv_sem.at[slot, h],
            device_id={"pts": target},
            device_id_type=MESH,
        )

    def along_layers(a, h):
        near = jnp.logical_or(
            jnp.logical_and(layer == 1, a == 0),
            jnp.logical_and(layer == layers - 2, a == layers - 1),
        )
        far = jnp.logical_or(
            jnp.logical_and(layer == 0, a == layers - 1),
            jnp.logical_and(layer == layers - 1, a == 0),
        )
        return jnp.logical_or(near, jnp.logical_and(far, h == PIECES - 1))

    def passes_up(a, h):
        near = jnp.logical_and(layer == 0, a == 0)
        far = jnp.logical_and(jnp.logical_and(layer == layers - 2, a == 0), h == PIECES - 1)
        return jnp.logical_and(layer < layers - 1, jnp.logical_or(near, far))

    def passes_down(a, h):
        near = jnp.logical_and(layer == layers - 1, a == layers - 1)
        far = jnp.logical_and(jnp.logical_and(layer == 1, a == layers - 1), h == PIECES - 1)
        return jnp.logical_and(layer > 0, jnp.logical_or(near, far))

    below, above = index(layer - 1, row, core), index(layer + 1, row, core)
    across, beside = index(layer, 1 - row, core), index(layer, row, 1 - core)

    mine = pl.ds(pl.multiple_of(grp * part, part), part)
    own = pl.ds(pl.multiple_of(me * part, part), part)
    gathered[own, :n_occ] = occ_ref[mine]
    gathered[own, n_occ:n_occ + n_vir] = vir_ref[mine]
    gathered[own, n_occ + n_vir:] = col_ref[mine]

    barrier = pltpu.get_barrier_semaphore()

    def greet(**where):
        pl.semaphore_signal(barrier, inc=1, device_id=where, device_id_type=MESH)

    greet(pts=across)
    greet(pts=beside)
    for step in range(1, groups):
        greet(grp=lax.rem(grp + step, groups))

    @pl.when(layer > 0)
    def _():
        greet(pts=below)

    @pl.when(layer < layers - 1)
    def _():
        greet(pts=above)

    ends = (layer == 0).astype(jnp.int32) + (layer == layers - 1).astype(jnp.int32)
    pl.semaphore_wait(barrier, groups + 3 - ends)

    for h in range(PIECES):
        @pl.when(layer > 0)
        def _():
            move(me, h, below, DOWN).start()

        @pl.when(layer < layers - 1)
        def _():
            move(me, h, above, UP).start()

        move(me, h, across, ACROSS).start()
        move(me, h, beside, BESIDE).start()

    total[...] = jnp.zeros_like(total)

    def scale(k, _):
        index_row = jnp.full((1, n_occ), tau_ref[k].astype(F32), F32)
        time = 0.05 * jnp.exp(index_row * jnp.float32(math.log(1.5)))
        rows = pl.ds(pl.multiple_of(k * points, points), points)
        decay = jnp.exp(occ_e_ref[...].reshape(1, n_occ) * time)
        occ_s[rows] = (occ_ref[...].astype(F32) * decay).astype(BF16)
        index_row = jnp.full((1, n_vir), tau_ref[k].astype(F32), F32)
        time = 0.05 * jnp.exp(index_row * jnp.float32(math.log(1.5)))
        decay = jnp.exp(-vir_e_ref[...].reshape(1, n_vir) * time)
        vir_s[rows] = (vir_ref[...].astype(F32) * decay).astype(BF16)
        for w in range(n_freq):
            cos_rows[w, k] = -weight_ref[k] * jnp.cos(freq_ref[w] * time[:, :pair])
        return 0

    lax.fori_loop(0, n_tau, scale, 0)

    def compute(a, b):
        slot = index(a, b, 0)
        rows = pl.ds(pl.multiple_of(slot * part, pair), pair)
        green_occ[...] = lax.dot_general(
            occ_s[...], gathered[rows, :n_occ], NT, preferred_element_type=F32
        )
        green_vir = lax.dot_general(
            vir_s[...], gathered[rows, n_occ:n_occ + n_vir], NT, preferred_element_type=F32
        )
        product = green_occ[...] * green_vir
        chi = []
        for w in range(n_freq):
            chi.append(
                sum(cos_rows[w, k] * product[k * points:(k + 1) * points] for k in range(n_tau))
            )
        lane = lax.broadcasted_iota(jnp.int32, (1, pair), 1)
        kept = jnp.where(
            lane < part,
            kept_ref[lax.rem(slot - me + cycle, cycle)].astype(F32),
            kept_ref[lax.rem(slot + 1 - me + cycle, cycle)].astype(F32),
        )
        for w in range(n_freq):
            masked = chi[w] * kept
            high = masked.astype(BF16)
            low = (masked - high.astype(F32)).astype(BF16)
            cols = gathered[rows, n_occ + n_vir:]
            total[w] += jnp.dot(high, cols, preferred_element_type=F32) + jnp.dot(
                low, cols, preferred_element_type=F32
            )

    def inside(a):
        return jnp.logical_and(a >= 0, a < layers)

    def same_row_arrives(t, h):
        for way in (-1, 1):
            @pl.when(inside(layer + way * t))
            def _():
                a = layer + way * t
                slot = index(a, row, core)
                move(slot, h, me, DOWN).wait_recv()
                onward = layer - way

                @pl.when(inside(onward))
                def _():
                    move(slot, h, index(onward, row, core), DOWN if way > 0 else UP).start()

                @pl.when(jnp.logical_not(along_layers(a, h)))
                def _():
                    move(slot, h, across, ACROSS).start()

                move(slot, h, beside, BESIDE).start()

    def other_row_arrives(t, h):
        for way in (-1, 1):
            @pl.when(jnp.logical_and(inside(layer + way * t), jnp.logical_or(t > 0, way > 0)))
            def _():
                a = layer + way * t
                slot = index(a, 1 - row, core)
                move(slot, h, me, DOWN).wait_recv()

                @pl.when(passes_up(a, h))
                def _():
                    move(slot, h, above, UP).start()

                @pl.when(passes_down(a, h))
                def _():
                    move(slot, h, below, DOWN).start()

                move(slot, h, beside, BESIDE).start()

    def work(a, b):
        for h in range(PIECES):
            move(index(a, b, 1 - core), h, me, DOWN).wait_recv()
        compute(a, b)

    def round_(t, _):
        def arrive(h, _):
            same_row_arrives(t, h)

            @pl.when(t > 0)
            def _():
                other_row_arrives(t - 1, h)
            return 0

        @pl.when(t > 0)
        def _():
            lax.fori_loop(0, PIECES, arrive, 0)

        def one(n, _):
            other = n // 2
            gap = t - other
            place = layer + gap * (2 * (n % 2) - 1)
            fresh = jnp.logical_or(gap > 0, jnp.logical_and(gap == 0, n % 2 == 1))

            @pl.when(jnp.logical_and(inside(place), fresh))
            def _():
                work(place, row + other * (1 - 2 * row))
            return 0

        lax.fori_loop(0, 4, one, 0)
        return 0

    lax.fori_loop(0, layers + 1, round_, 0)

    for w in range(n_freq):
        flipped = total[w].T
        turned[w] = flipped
        turned_sent[w] = flipped.astype(BF16)
    sums = []
    for step in range(1, groups):
        to = lax.rem(grp + step, groups)
        sums.append(
            pltpu.make_async_remote_copy(
                src_ref=turned_sent.at[:, pl.ds(pl.multiple_of(to * share, share), share)],
                dst_ref=landed.at[step - 1],
                send_sem=sum_send_sem.at[step - 1],
                recv_sem=sum_recv_sem.at[step - 1],
                device_id={"grp": to},
                device_id_type=MESH,
            )
        )
        sums[-1].start()

    def left(n, _):
        slot, h = n // PIECES, n % PIECES
        a, b, c = slot // (ROWS * CORES), (slot // CORES) % ROWS, slot % CORES

        @pl.when(c == core)
        def _():
            same, other = b == row, b != row
            down = jnp.logical_and(same, jnp.logical_and(a >= layer, layer > 0))
            up = jnp.logical_and(same, jnp.logical_and(a <= layer, layer < layers - 1))

            @pl.when(jnp.logical_or(down, jnp.logical_and(other, passes_down(a, h))))
            def _():
                move(slot, h, below, DOWN).wait_send()

            @pl.when(jnp.logical_or(up, jnp.logical_and(other, passes_up(a, h))))
            def _():
                move(slot, h, above, UP).wait_send()

            @pl.when(jnp.logical_and(same, jnp.logical_not(along_layers(a, h))))
            def _():
                move(slot, h, across, ACROSS).wait_send()

            move(slot, h, beside, BESIDE).wait_send()
        return 0

    lax.fori_loop(0, cycle * PIECES, left, 0)
    for copy in sums:
        copy.wait()
    answer = turned[:, pl.ds(pl.multiple_of(grp * share, share), share)]
    for step in range(groups - 1):
        answer = answer + landed[step].astype(F32)
    out_ref[...] = answer


def per_device(occ, vir, col, occ_e, vir_e, tau, weights, frequencies, kept):
    cycle, groups = lax.axis_size("pts"), lax.axis_size("grp")
    points, n_occ = occ.shape
    n_vir, n_col = vir.shape[1], col.shape[1]
    n_tau, n_freq = tau.shape[0], frequencies.shape[0]
    part, share = points // groups, n_col // groups
    vmem = pl.BlockSpec(memory_space=pltpu.VMEM)
    smem = pl.BlockSpec(memory_space=pltpu.SMEM)
    return pl.pallas_call(
        functools.partial(kernel, cycle, groups),
        out_shape=jax.ShapeDtypeStruct((n_freq, share, points), F32),
        in_specs=[vmem] * 5 + [smem] * 4,
        out_specs=vmem,
        scratch_shapes=[
            pltpu.VMEM((n_tau * points, n_occ), BF16),
            pltpu.VMEM((n_tau * points, n_vir), BF16),
            pltpu.VMEM((cycle * part, n_occ + n_vir + n_col), BF16),
            pltpu.VMEM((n_tau * points, CORES * part), F32),
            pltpu.VMEM((n_freq, points, n_col), F32),
            pltpu.VMEM((n_freq, n_col, points), F32),
            pltpu.VMEM((n_freq, n_col, points), BF16),
            pltpu.VMEM((groups - 1, n_freq, share, points), BF16),
            pltpu.VMEM((n_freq, n_tau, 1, CORES * part), F32),
            pltpu.SemaphoreType.DMA((4, cycle, PIECES)),
            pltpu.SemaphoreType.DMA((cycle, PIECES)),
            pltpu.SemaphoreType.DMA((groups - 1,)),
            pltpu.SemaphoreType.DMA((groups - 1,)),
        ],
        compiler_params=pltpu.CompilerParams(
            collective_id=0, has_side_effects=True, vmem_limit_bytes=56 * 1024 * 1024
        ),
    )(occ, vir, col, occ_e, vir_e, tau, weights, frequencies, kept)


def solution(mesh):
    placed = (P("pts", None), P("pts", None), P("pts", None), P(), P(), P(), P(), P(), P())
    return jax.shard_map(
        per_device, mesh=mesh, in_specs=placed, out_specs=P(None, "grp", "pts"), check_vma=False
    )
```
